32 devices in a mesh: energy: 8 (over z, y), space: 4 (over x, core).
Axes of the slice: x: 2, y: 2, z: 4, core: 2. Of those that a mesh axis runs over, the one named last changes fastest.
Arguments:
- iso_green: bfloat16 [8, 8, 2, 192, 192], P('energy', 'space'), as said below
- coupling: bfloat16 [8, 192, 192], P('space')
- screened: bfloat16 [8, 8, 2, 192, 192], P('energy', 'space'), as said below
Outputs:
- sigma: bfloat16 [8, 8, 2, 192, 192], P('energy', 'space')
Inputs may be any that keep to these rules, and one draw needn't show every extreme that they name: `iso_green`: every complex [192, 192] block (real and imaginary parts) equals its own transpose. `screened`: every complex [192, 192] block (real and imaginary parts) equals its own transpose.
All inputs are finite; a program needn't handle non-finite values.
Results may differ from the reference program's by a relative error of at most 0.023.
Values may be sent and summed in bfloat16 or wider, within the bound.
A program may use at most 64 MiB of HBM per device.

```python
import math
import jax
import jax.numpy as jnp
from jax import lax

B = 192
NE = 8
NBLK = 8


def draw_iso_green(key, part):
    key_own = jax.random.fold_in(key, 11)
    key_off, key_mag, key_phase = jax.random.split(key_own, 3)
    random_part = jax.random.normal(key_off, (NE, NBLK, 2, B, B), jnp.float32)
    magnitude = jnp.exp(jax.random.uniform(key_mag, (NE, NBLK, B), jnp.float32, math.log(0.85), math.log(0.97)))
    offdiag = (random_part + jnp.swapaxes(random_part, -1, -2)) * (0.15 / math.sqrt(2.0 * B))
    phases = jax.random.uniform(key_phase, (NE, NBLK, B), jnp.float32, -math.pi, 0.0)
    diagonal = jnp.stack([magnitude * jnp.cos(phases), magnitude * jnp.sin(phases)], axis=2)
    identity = jnp.eye(B, dtype=jnp.float32)
    return (offdiag + diagonal[..., None] * identity).astype(jnp.bfloat16)


def draw_coupling(key, part):
    key_own = jax.random.fold_in(key, 23)
    random_part = jax.random.normal(key_own, (NBLK, B, B), jnp.float32)
    identity = jnp.eye(B, dtype=jnp.float32)
    return (identity + random_part * (0.2 / math.sqrt(B))).astype(jnp.bfloat16)


def draw_screened(key, part):
    key_own = jax.random.fold_in(key, 37)
    random_part = jax.random.normal(key_own, (NE, NBLK, 2, B, B), jnp.float32)
    symmetric = (random_part + jnp.swapaxes(random_part, -1, -2)) * (0.05 * math.sqrt(B) / math.sqrt(2.0))
    return symmetric.astype(jnp.bfloat16)


def setup_inputs(seed: int = 0) -> dict:
    key_of = jax.random.split(jax.random.key(seed), 4)
    iso_green = draw_iso_green(jax.random.fold_in(key_of[3], 71), 0)
    coupling = draw_coupling(jax.random.fold_in(key_of[3], 71), 0)
    screened = draw_screened(jax.random.fold_in(key_of[3], 71), 0)
    return dict(iso_green=iso_green, coupling=coupling, screened=screened)


def complex_product(operand, factor, pattern):
    op_re = operand[:, 0].astype(jnp.float32)
    op_im = operand[:, 1].astype(jnp.float32)
    fa_re = factor[:, 0].astype(jnp.float32)
    fa_im = factor[:, 1].astype(jnp.float32)
    highest = lax.Precision.HIGHEST
    product_re = jnp.einsum(pattern, op_re, fa_re, precision=highest) - jnp.einsum(pattern, op_im, fa_im, precision=highest)
    product_im = jnp.einsum(pattern, op_re, fa_im, precision=highest) + jnp.einsum(pattern, op_im, fa_re, precision=highest)
    return jnp.stack([product_re, product_im], axis=1)

def sandwich(carried, factor, source):
    middle = complex_product(carried, factor, 'ekl,eml->ekm').astype(jnp.bfloat16)
    return (source.astype(jnp.float32) + complex_product(factor, middle, 'ekl,elm->ekm')).astype(jnp.bfloat16)

def chain_step(carried, inputs):
    updated = sandwich(carried, inputs[0], inputs[1])
    return (updated, updated)

def convolve_block(operands):
    green_block, screen_block = operands
    green_c = lax.complex(green_block[:, 0].astype(jnp.float32), green_block[:, 1].astype(jnp.float32))
    screen_c = lax.complex(screen_block[:, 0].astype(jnp.float32), screen_block[:, 1].astype(jnp.float32))
    spectrum = jnp.fft.fft(green_c, axis=0) * jnp.fft.fft(screen_c, axis=0)
    convolved = jnp.fft.ifft(spectrum, axis=0) / math.sqrt(NE)
    return jnp.stack([-jnp.imag(convolved), jnp.real(convolved)], axis=1).astype(jnp.bfloat16)

def reference(iso_green, coupling, screened):
    green_blocks = jnp.moveaxis(iso_green, 1, 0)
    transfer_blocks = jnp.einsum('ebckl,blm->beckm', iso_green.astype(jnp.float32), coupling.astype(jnp.float32), precision=lax.Precision.HIGHEST).astype(jnp.bfloat16)
    starting = jnp.zeros((NE, 2, B, B), jnp.bfloat16)
    connected = lax.scan(chain_step, starting, (transfer_blocks, green_blocks))[1]
    screen_blocks = jnp.moveaxis(screened, 1, 0)
    sigma_blocks = lax.map(convolve_block, (connected, screen_blocks))
    return jnp.moveaxis(sigma_blocks, 0, 1)
```

```python
import functools
import math

import jax
import jax.numpy as jnp
from jax import lax
from jax.experimental import pallas as pl
from jax.experimental.pallas import tpu as pltpu
from jax.sharding import PartitionSpec as P

MESH = pl.DeviceIdType.MESH
BF16 = jnp.bfloat16
F32 = jnp.float32
UNROLL = 8


def loop(low, high, body):
    if high - low <= UNROLL:
        for step in range(low, high):
            body(step)
    else:

        def one(step, carry):
            body(step)
            return carry

        lax.fori_loop(low, high, one, 0)


def dot(a, b):
    return jnp.dot(a, b, preferred_element_type=F32)


def dot_tn(a, b):
    return lax.dot_general(a, b, (((0,), (0,)), ((), ())), preferred_element_type=F32)


def product(a, b, mul=dot):
    real = mul(a[0], b[0]) - mul(a[1], b[1])
    imag = mul(a[0], b[1]) + mul(a[1], b[0])
    return real, imag


def rounded(pair):
    return pair[0].astype(BF16), pair[1].astype(BF16)


def load(ref, *at):
    return ref[(*at, 0)], ref[(*at, 1)]


def store(ref, pair, *at):
    ref[(*at, 0)] = pair[0].astype(BF16)
    ref[(*at, 1)] = pair[1].astype(BF16)


def sandwich(source, left, inner, right):
    outer = product(left, rounded(product(inner, right)))
    return source[0].astype(F32) + outer[0], source[1].astype(F32) + outer[1]


def pack(ref, plane, start, whole):
    t = whole.shape[0] // 3
    ref[plane, start : start + t] = whole[2 * t :, : 2 * t].astype(BF16)
    ref[plane, start + t : start + 2 * t] = whole[:t, : 2 * t].astype(BF16)
    corner = jnp.concatenate([whole[2 * t :, 2 * t :], whole[t : 2 * t, t : 2 * t]], axis=1)
    ref[plane, start + 2 * t : start + 3 * t] = corner.astype(BF16)


def unpack(ref, at, rows):
    t = rows.shape[0] // 3
    low, top, corner = rows[:t], rows[t : 2 * t], rows[2 * t :]
    flipped = top.astype(F32).T[t:].astype(BF16)
    ref[(*at, slice(2 * t, 3 * t), slice(0, 2 * t))] = low
    ref[(*at, slice(2 * t, 3 * t), slice(2 * t, 3 * t))] = corner[:, :t]
    ref[(*at, slice(0, t), slice(0, 2 * t))] = top
    ref[(*at, slice(t, 2 * t), slice(0, 2 * t))] = jnp.concatenate(
        [flipped, corner[:, t:]], axis=1
    )
    ref[(*at, slice(0, 2 * t), slice(2 * t, 3 * t))] = low.astype(F32).T.astype(BF16)


def kernel(
    groups,
    places,
    iso_ref,
    coupling_ref,
    screened_ref,
    out_ref,
    green,
    hop,
    screen,
    maps,
    maps_t,
    conn,
    pair_conn,
    pair_map,
    carry_packed,
    carry,
    green_send,
    screen_send,
    green_recv,
    screen_recv,
    green_wide,
    screen_wide,
    sigma_send,
    sigma_recv,
    load_sem,
    pair_sem,
    carry_sem,
    trade_sem,
    exchange_sem,
):
    blocks = green.shape[0]
    order = green.shape[-1]
    chunk = green_recv.shape[2]
    last = blocks - 1
    me = lax.axis_index("energy")
    place = lax.axis_index("space")
    pair = place // 2
    side = place % 2
    odd = side == 1
    partner = place + 1 - 2 * side
    pairs = places // 2

    loads = [
        pltpu.make_async_copy(iso_ref.at[0], green, load_sem.at[0]),
        pltpu.make_async_copy(coupling_ref, hop, load_sem.at[1]),
        pltpu.make_async_copy(screened_ref.at[0], screen, load_sem.at[2]),
    ]
    for copy in loads:
        copy.start()

    barrier = pltpu.get_barrier_semaphore()

    def greet(step):
        pl.semaphore_signal(
            barrier, inc=1, device_id={"energy": (me + step) % groups}, device_id_type=MESH
        )

    loop(1, groups, greet)
    pl.semaphore_signal(barrier, inc=1, device_id={"space": partner}, device_id_type=MESH)
    sends_on = jnp.logical_and(odd, pair < pairs - 1)

    @pl.when(sends_on)
    def _():
        for plane in range(2):
            pl.semaphore_signal(
                barrier, inc=1, device_id={"space": place + 1 + plane}, device_id_type=MESH
            )

    @pl.when(pair > 0)
    def _():
        pl.semaphore_signal(barrier, inc=1, device_id={"space": 2 * pair - 1}, device_id_type=MESH)

    def exchange(index, source, target, step):
        to = (me + step) % groups
        return pltpu.make_async_remote_copy(
            src_ref=source(to),
            dst_ref=target,
            send_sem=exchange_sem.at[2 * index],
            recv_sem=exchange_sem.at[2 * index + 1],
            device_id={"energy": to},
            device_id_type=MESH,
        )

    def spread(ref):
        return lambda to: ref.at[:, pl.ds(pl.multiple_of(to * chunk, 16), chunk), :]

    def whole(index):
        part = green_recv.at[pl.ds(0, groups - 1)]
        return pltpu.make_async_remote_copy(
            src_ref=part,
            dst_ref=part,
            send_sem=exchange_sem.at[2 * index],
            recv_sem=exchange_sem.at[2 * index + 1],
            device_id={"energy": (me + 1) % groups},
            device_id_type=MESH,
        )

    pair_copies = [
        pltpu.make_async_remote_copy(
            src_ref=source,
            dst_ref=target,
            send_sem=pair_sem.at[2 * index],
            recv_sem=pair_sem.at[2 * index + 1],
            device_id={"space": partner},
            device_id_type=MESH,
        )
        for index, (source, target) in enumerate(
            [(conn.at[last], pair_conn), (maps.at[last], pair_map)]
        )
    ]

    def onward(plane):
        return pltpu.make_async_remote_copy(
            src_ref=green_send.at[plane, last * order : blocks * order],
            dst_ref=carry_packed.at[plane],
            send_sem=carry_sem.at[plane],
            recv_sem=carry_sem.at[2],
            device_id={"space": place + 1 + plane},
            device_id_type=MESH,
        )

    trade = pltpu.make_async_remote_copy(
        src_ref=carry_packed.at[side],
        dst_ref=carry_packed.at[side],
        send_sem=trade_sem.at[0],
        recv_sem=trade_sem.at[1],
        device_id={"space": partner},
        device_id_type=MESH,
    )

    loads[0].wait()
    loads[1].wait()

    def steps_of(block):
        kept = load(green, block)
        hopping = hop[block]
        ahead = (dot(kept[0], hopping).astype(BF16), dot(kept[1], hopping).astype(BF16))
        behind = (dot_tn(hopping, kept[0]).astype(BF16), dot_tn(hopping, kept[1]).astype(BF16))
        return ahead, behind

    store(conn, load(green, 0), 0)
    for block in range(1, blocks):
        ahead, behind = steps_of(block)
        store(maps, ahead, block)
        store(maps_t, behind, block)
        store(
            conn, sandwich(load(green, block), ahead, load(conn, block - 1), behind), block
        )

    pl.semaphore_wait(
        barrier,
        groups
        + 2 * jnp.where(sends_on, 1, 0).astype(jnp.int32)
        + jnp.where(pair > 0, 1, 0).astype(jnp.int32),
    )

    @pl.when(side == 0)
    def _():
        pair_copies[0].start()

    @pl.when(jnp.logical_or(odd, pair > 0))
    def _():
        ahead, behind = steps_of(0)
        store(maps, ahead, 0)
        store(maps_t, behind, 0)
        for block in range(1, blocks):
            before, before_t = load(maps, block - 1), load(maps_t, block - 1)
            ahead, behind = load(maps, block), load(maps_t, block)
            store(maps, product(ahead, before), block)
            store(maps_t, product(before_t, behind), block)

    @pl.when(jnp.logical_and(side == 0, pair > 0))
    def _():
        pair_copies[1].start()

    loads[2].wait()
    for block in range(blocks):
        for plane in range(2):
            pack(screen_send, plane, block * order, screen[block, plane])
    used = blocks * order
    if groups * chunk > used:
        for ref in (screen_send, green_send):
            ref[:, used:] = jnp.zeros((2, groups * chunk - used, ref.shape[2]), BF16)
    loop(
        1, groups, lambda step: exchange(0, spread(screen_send), screen_recv.at[me], step).start()
    )

    @pl.when(odd)
    def _():
        pair_copies[0].wait_recv()
        below = load(pair_conn)
        for block in reversed(range(blocks)):
            ahead, behind = load(maps, block), load(maps_t, block)
            store(conn, sandwich(load(conn, block), ahead, below, behind), block)

        @pl.when(pair > 0)
        def _():
            pair_copies[1].wait_recv()
            before = load(pair_map)
            for block in range(blocks):
                ahead, behind = load(maps, block), load(maps_t, block)
                store(maps, product(ahead, before), block)
                store(maps_t, product(before, behind, dot_tn), block)

    @pl.when(side == 0)
    def _():
        pair_copies[0].wait_send()

        @pl.when(pair > 0)
        def _():
            pair_copies[1].wait_send()

    @pl.when(pair > 0)
    def _():
        pltpu.make_async_remote_copy(
            src_ref=carry_packed.at[side],
            dst_ref=carry_packed.at[side],
            send_sem=carry_sem.at[0],
            recv_sem=carry_sem.at[2],
            device_id={"space": partner},
            device_id_type=MESH,
        ).wait_recv()
        trade.start()
        trade.wait()
        for plane in range(2):
            unpack(carry, (plane,), carry_packed[plane])

    for block in reversed(range(blocks)):

        @pl.when(pair > 0)
        def _():
            ahead, behind = load(maps, block), load(maps_t, block)
            store(conn, sandwich(load(conn, block), ahead, load(carry), behind), block)

        for plane in range(2):
            pack(green_send, plane, block * order, conn[block, plane])
        if block == last:

            @pl.when(sends_on)
            def _():
                for plane in range(2):
                    onward(plane).start()

    loop(1, groups, lambda step: exchange(1, spread(green_send), green_recv.at[me], step).start())
    mine = pl.ds(pl.multiple_of(me * chunk, 16), chunk)
    green_recv[me] = green_send[:, mine]
    screen_recv[me] = screen_send[:, mine]

    whole(0).wait_recv()

    def widen_screen(energy):
        screen_wide[energy] = screen_recv[energy].astype(F32)

    def widen_green(energy):
        green_wide[energy] = green_recv[energy].astype(F32)

    loop(0, groups, widen_screen)
    whole(1).wait_recv()
    loop(0, groups, widen_green)
    scale = 1.0 / math.sqrt(groups)

    def convolved(energy):
        def term(other, total):
            shift = (energy - other + groups) % groups
            g_re, g_im = green_wide[other, 0], green_wide[other, 1]
            s_re, s_im = screen_wide[shift, 0], screen_wide[shift, 1]
            return (
                total[0] + g_re * s_re - g_im * s_im,
                total[1] + g_re * s_im + g_im * s_re,
            )

        zero = jnp.zeros(green_wide.shape[2:], F32)
        total = (zero, zero)
        if groups <= UNROLL:
            for other in range(groups):
                total = term(other, total)
        else:
            total = lax.fori_loop(0, groups, term, total)
        return (total[1] * -scale).astype(BF16), (total[0] * scale).astype(BF16)

    def back(step):
        energy = (me + step) % groups
        real, imag = convolved(energy)
        sigma_send[step, 0] = real
        sigma_send[step, 1] = imag
        exchange(2, lambda to: sigma_send.at[step], spread(sigma_recv)(me), step).start()

    loop(1, groups, back)
    real, imag = convolved(me)
    sigma_recv[0, mine] = real
    sigma_recv[1, mine] = imag
    whole(2).wait_recv()
    for block in range(blocks):
        for plane in range(2):
            unpack(
                out_ref, (0, block, plane), sigma_recv[plane, block * order : (block + 1) * order]
            )

    for index in range(3):
        whole(index).wait_send()

    @pl.when(sends_on)
    def _():
        for plane in range(2):
            onward(plane).wait_send()


def shards(groups, places, iso_green, coupling, screened):
    blocks, order = iso_green.shape[1], iso_green.shape[3]
    tile = order // 3
    width = 2 * tile
    used = blocks * order
    chunk = 16 * -(-used // (16 * groups))
    full = (2, order, order)
    any_spec = pl.BlockSpec(memory_space=pl.ANY)
    return pl.pallas_call(
        functools.partial(kernel, groups, places),
        out_shape=jax.ShapeDtypeStruct(iso_green.shape, BF16),
        in_specs=[any_spec] * 3,
        out_specs=pl.BlockSpec(memory_space=pltpu.VMEM),
        scratch_shapes=[
            pltpu.VMEM((blocks, *full), BF16),
            pltpu.VMEM((blocks, order, order), BF16),
            pltpu.VMEM((blocks, *full), BF16),
            pltpu.VMEM((blocks, *full), BF16),
            pltpu.VMEM((blocks, *full), BF16),
            pltpu.VMEM((blocks, *full), BF16),
            pltpu.VMEM(full, BF16),
            pltpu.VMEM(full, BF16),
            pltpu.VMEM((2, order, width), BF16),
            pltpu.VMEM(full, BF16),
            pltpu.VMEM((2, groups * chunk, width), BF16),
            pltpu.VMEM((2, groups * chunk, width), BF16),
            pltpu.VMEM((groups, 2, chunk, width), BF16),
            pltpu.VMEM((groups, 2, chunk, width), BF16),
            pltpu.VMEM((groups, 2, chunk, width), F32),
            pltpu.VMEM((groups, 2, chunk, width), F32),
            pltpu.VMEM((groups, 2, chunk, width), BF16),
            pltpu.VMEM((2, groups * chunk, width), BF16),
            pltpu.SemaphoreType.DMA((3,)),
            pltpu.SemaphoreType.DMA((4,)),
            pltpu.SemaphoreType.DMA((3,)),
            pltpu.SemaphoreType.DMA((2,)),
            pltpu.SemaphoreType.DMA((6,)),
        ],
        compiler_params=pltpu.CompilerParams(
            collective_id=0, has_side_effects=True, vmem_limit_bytes=32 * 1024 * 1024
        ),
    )(iso_green, coupling, screened)


def solution(mesh):
    groups, places = mesh.shape["energy"], mesh.shape["space"]
    spec = P("energy", "space", None, None, None)
    return jax.shard_map(
        functools.partial(shards, groups, places),
        mesh=mesh,
        in_specs=(spec, P("space", None, None), spec),
        out_specs=spec,
        check_vma=False,
    )
```

```python
import functools
import math

import jax
import jax.numpy as jnp
from jax import lax
from jax.experimental import pallas as pl
from jax.experimental.pallas import tpu as pltpu
from jax.sharding import PartitionSpec as P

MESH = pl.DeviceIdType.MESH
BF16 = jnp.bfloat16
F32 = jnp.float32
UNROLL = 8


def loop(low, high, body):
    if high - low <= UNROLL:
        for step in range(low, high):
            body(step)
    else:

        def one(step, carry):
            body(step)
            return carry

        lax.fori_loop(low, high, one, 0)


def dot(a, b):
    return jnp.dot(a, b, preferred_element_type=F32)


def dot_tn(a, b):
    return lax.dot_general(a, b, (((0,), (0,)), ((), ())), preferred_element_type=F32)


def product(a, b, mul=dot):
    real = mul(a[0], b[0]) - mul(a[1], b[1])
    imag = mul(a[0], b[1]) + mul(a[1], b[0])
    return real, imag


def rounded(pair):
    return pair[0].astype(BF16), pair[1].astype(BF16)


def load(ref, *at):
    return ref[(*at, 0)], ref[(*at, 1)]


def store(ref, pair, *at):
    ref[(*at, 0)] = pair[0].astype(BF16)
    ref[(*at, 1)] = pair[1].astype(BF16)


def sandwich(source, left, inner, right):
    outer = product(left, rounded(product(inner, right)))
    return source[0].astype(F32) + outer[0], source[1].astype(F32) + outer[1]


def pack(ref, plane, start, whole):
    t = whole.shape[0] // 3
    ref[plane, start : start + t] = whole[2 * t :, : 2 * t].astype(BF16)
    ref[plane, start + t : start + 2 * t] = whole[:t, : 2 * t].astype(BF16)
    corner = jnp.concatenate([whole[2 * t :, 2 * t :], whole[t : 2 * t, t : 2 * t]], axis=1)
    ref[plane, start + 2 * t : start + 3 * t] = corner.astype(BF16)


def unpack(ref, at, rows):
    t = rows.shape[0] // 3
    low, top, corner = rows[:t], rows[t : 2 * t], rows[2 * t :]
    flipped = top.astype(F32).T[t:].astype(BF16)
    ref[(*at, slice(2 * t, 3 * t), slice(0, 2 * t))] = low
    ref[(*at, slice(2 * t, 3 * t), slice(2 * t, 3 * t))] = corner[:, :t]
    ref[(*at, slice(0, t), slice(0, 2 * t))] = top
    ref[(*at, slice(t, 2 * t), slice(0, 2 * t))] = jnp.concatenate(
        [flipped, corner[:, t:]], axis=1
    )
    ref[(*at, slice(0, 2 * t), slice(2 * t, 3 * t))] = low.astype(F32).T.astype(BF16)


def kernel(
    groups,
    places,
    iso_ref,
    coupling_ref,
    screened_ref,
    out_ref,
    green,
    hop,
    screen,
    maps,
    maps_t,
    conn,
    pair_conn,
    pair_map,
    carry_packed,
    carry,
    green_send,
    screen_send,
    green_recv,
    screen_recv,
    green_wide,
    screen_wide,
    sigma_send,
    sigma_recv,
    load_sem,
    pair_sem,
    carry_sem,
    trade_sem,
    exchange_sem,
):
    blocks = green.shape[0]
    order = green.shape[-1]
    chunk = green_recv.shape[2]
    last = blocks - 1
    me = lax.axis_index("energy")
    place = lax.axis_index("space")
    pair = place // 2
    side = place % 2
    odd = side == 1
    partner = place + 1 - 2 * side
    pairs = places // 2

    loads = [
        pltpu.make_async_copy(iso_ref.at[0], green, load_sem.at[0]),
        pltpu.make_async_copy(coupling_ref, hop, load_sem.at[1]),
        pltpu.make_async_copy(screened_ref.at[0], screen, load_sem.at[2]),
    ]
    for copy in loads:
        copy.start()

    barrier = pltpu.get_barrier_semaphore()

    def greet(step):
        pl.semaphore_signal(
            barrier, inc=1, device_id={"energy": (me + step) % groups}, device_id_type=MESH
        )

    loop(1, groups, greet)
    pl.semaphore_signal(barrier, inc=1, device_id={"space": partner}, device_id_type=MESH)
    sends_on = jnp.logical_and(odd, pair < pairs - 1)

    @pl.when(sends_on)
    def _():
        for plane in range(2):
            pl.semaphore_signal(
                barrier, inc=1, device_id={"space": place + 1 + plane}, device_id_type=MESH
            )

    @pl.when(pair > 0)
    def _():
        pl.semaphore_signal(barrier, inc=1, device_id={"space": 2 * pair - 1}, device_id_type=MESH)

    def exchange(index, source, target, step):
        to = (me + step) % groups
        return pltpu.make_async_remote_copy(
            src_ref=source(to),
            dst_ref=target,
            send_sem=exchange_sem.at[2 * index],
            recv_sem=exchange_sem.at[2 * index + 1],
            device_id={"energy": to},
            device_id_type=MESH,
        )

    def spread(ref):
        return lambda to: ref.at[:, pl.ds(pl.multiple_of(to * chunk, 16), chunk), :]

    def whole(index):
        part = green_recv.at[pl.ds(0, groups - 1)]
        return pltpu.make_async_remote_copy(
            src_ref=part,
            dst_ref=part,
            send_sem=exchange_sem.at[2 * index],
            recv_sem=exchange_sem.at[2 * index + 1],
            device_id={"energy": (me + 1) % groups},
            device_id_type=MESH,
        )

    pair_copies = [
        pltpu.make_async_remote_copy(
            src_ref=source,
            dst_ref=target,
            send_sem=pair_sem.at[2 * index],
            recv_sem=pair_sem.at[2 * index + 1],
            device_id={"space": partner},
            device_id_type=MESH,
        )
        for index, (source, target) in enumerate(
            [(conn.at[last], pair_conn), (maps.at[last], pair_map)]
        )
    ]

    def onward(plane):
        return pltpu.make_async_remote_copy(
            src_ref=green_send.at[plane, last * order : blocks * order],
            dst_ref=carry_packed.at[plane],
            send_sem=carry_sem.at[plane],
            recv_sem=carry_sem.at[2],
            device_id={"space": place + 1 + plane},
            device_id_type=MESH,
        )

    trade = pltpu.make_async_remote_copy(
        src_ref=carry_packed.at[side],
        dst_ref=carry_packed.at[side],
        send_sem=trade_sem.at[0],
        recv_sem=trade_sem.at[1],
        device_id={"space": partner},
        device_id_type=MESH,
    )

    loads[0].wait()
    loads[1].wait()

    def steps_of(block):
        kept = load(green, block)
        hopping = hop[block]
        ahead = (dot(kept[0], hopping).astype(BF16), dot(kept[1], hopping).astype(BF16))
        behind = (dot_tn(hopping, kept[0]).astype(BF16), dot_tn(hopping, kept[1]).astype(BF16))
        return ahead, behind

    store(conn, load(green, 0), 0)
    for block in range(1, blocks):
        ahead, behind = steps_of(block)
        store(maps, ahead, block)
        store(maps_t, behind, block)
        store(
            conn, sandwich(load(green, block), ahead, load(conn, block - 1), behind), block
        )

    pl.semaphore_wait(
        barrier,
        groups
        + 2 * jnp.where(sends_on, 1, 0).astype(jnp.int32)
        + jnp.where(pair > 0, 1, 0).astype(jnp.int32),
    )

    @pl.when(side == 0)
    def _():
        pair_copies[0].start()

    @pl.when(jnp.logical_or(odd, pair > 0))
    def _():
        ahead, behind = steps_of(0)
        store(maps, ahead, 0)
        store(maps_t, behind, 0)
        for block in range(1, blocks):
            before, before_t = load(maps, block - 1), load(maps_t, block - 1)
            ahead, behind = load(maps, block), load(maps_t, block)
            store(maps, product(ahead, before), block)
            store(maps_t, product(before_t, behind), block)

    @pl.when(jnp.logical_and(side == 0, pair > 0))
    def _():
        pair_copies[1].start()

    loads[2].wait()
    for block in range(blocks):
        for plane in range(2):
            pack(screen_send, plane, block * order, screen[block, plane])
    used = blocks * order
    if groups * chunk > used:
        for ref in (screen_send, green_send):
            ref[:, used:] = jnp.zeros((2, groups * chunk - used, ref.shape[2]), BF16)
    loop(
        1, groups, lambda step: exchange(0, spread(screen_send), screen_recv.at[me], step).start()
    )

    @pl.when(odd)
    def _():
        pair_copies[0].wait_recv()
        below = load(pair_conn)
        for block in reversed(range(blocks)):
            ahead, behind = load(maps, block), load(maps_t, block)
            store(conn, sandwich(load(conn, block), ahead, below, behind), block)

        @pl.when(pair > 0)
        def _():
            pair_copies[1].wait_recv()
            before = load(pair_map)
            for block in range(blocks):
                ahead, behind = load(maps, block), load(maps_t, block)
                store(maps, product(ahead, before), block)
                store(maps_t, product(before, behind, dot_tn), block)

    @pl.when(pair > 0)
    def _():
        @pl.when(side == 0)
        def _():
            pair_copies[0].wait_send()
            pair_copies[1].wait_send()

        pltpu.make_async_remote_copy(
            src_ref=carry_packed.at[side],
            dst_ref=carry_packed.at[side],
            send_sem=carry_sem.at[0],
            recv_sem=carry_sem.at[2],
            device_id={"space": partner},
            device_id_type=MESH,
        ).wait_recv()
        trade.start()
        trade.wait()
        for plane in range(2):
            unpack(carry, (plane,), carry_packed[plane])

    for block in reversed(range(blocks)):

        @pl.when(pair > 0)
        def _():
            ahead, behind = load(maps, block), load(maps_t, block)
            store(conn, sandwich(load(conn, block), ahead, load(carry), behind), block)

        for plane in range(2):
            pack(green_send, plane, block * order, conn[block, plane])
        if block == last:

            @pl.when(sends_on)
            def _():
                for plane in range(2):
                    onward(plane).start()

    loop(1, groups, lambda step: exchange(1, spread(green_send), green_recv.at[me], step).start())
    mine = pl.ds(pl.multiple_of(me * chunk, 16), chunk)
    green_recv[me] = green_send[:, mine]
    screen_recv[me] = screen_send[:, mine]

    whole(0).wait_recv()

    def widen_screen(energy):
        screen_wide[energy] = screen_recv[energy].astype(F32)

    def widen_green(energy):
        green_wide[energy] = green_recv[energy].astype(F32)

    loop(0, groups, widen_screen)
    whole(1).wait_recv()
    loop(0, groups, widen_green)
    scale = 1.0 / math.sqrt(groups)

    def convolved(energy):
        def term(other, total):
            shift = (energy - other + groups) % groups
            g_re, g_im = green_wide[other, 0], green_wide[other, 1]
            s_re, s_im = screen_wide[shift, 0], screen_wide[shift, 1]
            return (
                total[0] + g_re * s_re - g_im * s_im,
                total[1] + g_re * s_im + g_im * s_re,
            )

        zero = jnp.zeros(green_wide.shape[2:], F32)
        total = (zero, zero)
        if groups <= UNROLL:
            for other in range(groups):
                total = term(other, total)
        else:
            total = lax.fori_loop(0, groups, term, total)
        return (total[1] * -scale).astype(BF16), (total[0] * scale).astype(BF16)

    def back(step):
        energy = (me + step) % groups
        real, imag = convolved(energy)
        sigma_send[step, 0] = real
        sigma_send[step, 1] = imag
        exchange(2, lambda to: sigma_send.at[step], spread(sigma_recv)(me), step).start()

    loop(1, groups, back)
    real, imag = convolved(me)
    sigma_recv[0, mine] = real
    sigma_recv[1, mine] = imag
    whole(2).wait_recv()
    for block in range(blocks):
        for plane in range(2):
            unpack(
                out_ref, (0, block, plane), sigma_recv[plane, block * order : (block + 1) * order]
            )

    for index in range(3):
        whole(index).wait_send()

    @pl.when(jnp.logical_and(side == 0, pair == 0))
    def _():
        pair_copies[0].wait_send()

    @pl.when(sends_on)
    def _():
        for plane in range(2):
            onward(plane).wait_send()


def shards(groups, places, iso_green, coupling, screened):
    blocks, order = iso_green.shape[1], iso_green.shape[3]
    tile = order // 3
    width = 2 * tile
    used = blocks * order
    chunk = 16 * -(-used // (16 * groups))
    full = (2, order, order)
    any_spec = pl.BlockSpec(memory_space=pltpu.HBM)
    return pl.pallas_call(
        functools.partial(kernel, groups, places),
        out_shape=jax.ShapeDtypeStruct(iso_green.shape, BF16),
        in_specs=[any_spec] * 3,
        out_specs=pl.BlockSpec(memory_space=pltpu.VMEM),
        scratch_shapes=[
            pltpu.VMEM((blocks, *full), BF16),
            pltpu.VMEM((blocks, order, order), BF16),
            pltpu.VMEM((blocks, *full), BF16),
            pltpu.VMEM((blocks, *full), BF16),
            pltpu.VMEM((blocks, *full), BF16),
            pltpu.VMEM((blocks, *full), BF16),
            pltpu.VMEM(full, BF16),
            pltpu.VMEM(full, BF16),
            pltpu.VMEM((2, order, width), BF16),
            pltpu.VMEM(full, BF16),
            pltpu.VMEM((2, groups * chunk, width), BF16),
            pltpu.VMEM((2, groups * chunk, width), BF16),
            pltpu.VMEM((groups, 2, chunk, width), BF16),
            pltpu.VMEM((groups, 2, chunk, width), BF16),
            pltpu.VMEM((groups, 2, chunk, width), F32),
            pltpu.VMEM((groups, 2, chunk, width), F32),
            pltpu.VMEM((groups, 2, chunk, width), BF16),
            pltpu.VMEM((2, groups * chunk, width), BF16),
            pltpu.SemaphoreType.DMA((3,)),
            pltpu.SemaphoreType.DMA((4,)),
            pltpu.SemaphoreType.DMA((3,)),
            pltpu.SemaphoreType.DMA((2,)),
            pltpu.SemaphoreType.DMA((6,)),
        ],
        compiler_params=pltpu.CompilerParams(
            collective_id=0, has_side_effects=True, vmem_limit_bytes=32 * 1024 * 1024
        ),
    )(iso_green, coupling, screened)


def solution(mesh):
    groups, places = mesh.shape["energy"], mesh.shape["space"]
    spec = P("energy", "space", None, None, None)
    return jax.shard_map(
        functools.partial(shards, groups, places),
        mesh=mesh,
        in_specs=(spec, P("space", None, None), spec),
        out_specs=spec,
        check_vma=False,
    )
```

```python
import functools
import math

import jax
import jax.numpy as jnp
from jax import lax
from jax.experimental import pallas as pl
from jax.experimental.pallas import tpu as pltpu
from jax.sharding import PartitionSpec as P

MESH = pl.DeviceIdType.MESH
BF16 = jnp.bfloat16
F32 = jnp.float32
UNROLL = 8


def loop(low, high, body):
    if high - low <= UNROLL:
        for step in range(low, high):
            body(step)
    else:

        def one(step, carry):
            body(step)
            return carry

        lax.fori_loop(low, high, one, 0)


def dot(a, b):
    return jnp.dot(a, b, preferred_element_type=F32)


def dot_tn(a, b):
    return lax.dot_general(a, b, (((0,), (0,)), ((), ())), preferred_element_type=F32)


def product(a, b, mul=dot):
    real = mul(a[0], b[0]) - mul(a[1], b[1])
    imag = mul(a[0], b[1]) + mul(a[1], b[0])
    return real, imag


def rounded(pair):
    return pair[0].astype(BF16), pair[1].astype(BF16)


def load(ref, *at):
    return ref[(*at, 0)], ref[(*at, 1)]


def store(ref, pair, *at):
    ref[(*at, 0)] = pair[0].astype(BF16)
    ref[(*at, 1)] = pair[1].astype(BF16)


def sandwich(source, left, inner, right):
    outer = product(left, rounded(product(inner, right)))
    return source[0].astype(F32) + outer[0], source[1].astype(F32) + outer[1]


def pack(ref, plane, start, whole):
    t = whole.shape[0] // 3
    ref[plane, start : start + t] = whole[2 * t :, : 2 * t].astype(BF16)
    ref[plane, start + t : start + 2 * t] = whole[:t, : 2 * t].astype(BF16)
    corner = jnp.concatenate([whole[2 * t :, 2 * t :], whole[t : 2 * t, t : 2 * t]], axis=1)
    ref[plane, start + 2 * t : start + 3 * t] = corner.astype(BF16)


def unpack(ref, at, rows):
    t = rows.shape[0] // 3
    low, top, corner = rows[:t], rows[t : 2 * t], rows[2 * t :]
    flipped = top.astype(F32).T[t:].astype(BF16)
    ref[(*at, slice(2 * t, 3 * t), slice(0, 2 * t))] = low
    ref[(*at, slice(2 * t, 3 * t), slice(2 * t, 3 * t))] = corner[:, :t]
    ref[(*at, slice(0, t), slice(0, 2 * t))] = top
    ref[(*at, slice(t, 2 * t), slice(0, 2 * t))] = jnp.concatenate(
        [flipped, corner[:, t:]], axis=1
    )
    ref[(*at, slice(0, 2 * t), slice(2 * t, 3 * t))] = low.astype(F32).T.astype(BF16)


def kernel(
    groups,
    places,
    iso_ref,
    coupling_ref,
    screened_ref,
    out_ref,
    green,
    hop,
    screen,
    maps,
    maps_t,
    conn,
    pair_conn,
    pair_map,
    carry_packed,
    carry,
    green_send,
    screen_send,
    green_recv,
    screen_recv,
    green_wide,
    screen_wide,
    sigma_send,
    sigma_recv,
    load_sem,
    pair_sem,
    carry_sem,
    trade_sem,
    exchange_sem,
):
    blocks = green.shape[0]
    order = green.shape[-1]
    chunk = green_recv.shape[2]
    last = blocks - 1
    me = lax.axis_index("energy")
    place = lax.axis_index("space")
    pair = place // 2
    side = place % 2
    odd = side == 1
    partner = place + 1 - 2 * side
    pairs = places // 2

    loads = [
        pltpu.make_async_copy(iso_ref.at[0], green, load_sem.at[0]),
        pltpu.make_async_copy(coupling_ref, hop, load_sem.at[1]),
        pltpu.make_async_copy(screened_ref.at[0], screen, load_sem.at[2]),
    ]
    for copy in loads:
        copy.start()

    barrier = pltpu.get_barrier_semaphore()

    def greet(step):
        pl.semaphore_signal(
            barrier, inc=1, device_id={"energy": (me + step) % groups}, device_id_type=MESH
        )

    loop(1, groups, greet)
    pl.semaphore_signal(barrier, inc=1, device_id={"space": partner}, device_id_type=MESH)
    sends_on = jnp.logical_and(odd, pair < pairs - 1)

    @pl.when(sends_on)
    def _():
        for plane in range(2):
            pl.semaphore_signal(
                barrier, inc=1, device_id={"space": place + 1 + plane}, device_id_type=MESH
            )

    @pl.when(pair > 0)
    def _():
        pl.semaphore_signal(barrier, inc=1, device_id={"space": 2 * pair - 1}, device_id_type=MESH)

    def exchange(index, source, target, step):
        to = (me + step) % groups
        return pltpu.make_async_remote_copy(
            src_ref=source(to),
            dst_ref=target,
            send_sem=exchange_sem.at[2 * index],
            recv_sem=exchange_sem.at[2 * index + 1],
            device_id={"energy": to},
            device_id_type=MESH,
        )

    def spread(ref):
        return lambda to: ref.at[:, pl.ds(pl.multiple_of(to * chunk, 16), chunk), :]

    def whole(index):
        part = green_recv.at[pl.ds(0, groups - 1)]
        return pltpu.make_async_remote_copy(
            src_ref=part,
            dst_ref=part,
            send_sem=exchange_sem.at[2 * index],
            recv_sem=exchange_sem.at[2 * index + 1],
            device_id={"energy": (me + 1) % groups},
            device_id_type=MESH,
        )

    pair_copies = [
        pltpu.make_async_remote_copy(
            src_ref=source,
            dst_ref=target,
            send_sem=pair_sem.at[2 * index],
            recv_sem=pair_sem.at[2 * index + 1],
            device_id={"space": partner},
            device_id_type=MESH,
        )
        for index, (source, target) in enumerate(
            [(conn.at[last], pair_conn), (maps.at[last], pair_map)]
        )
    ]

    def onward(plane):
        return pltpu.make_async_remote_copy(
            src_ref=green_send.at[plane, last * order : blocks * order],
            dst_ref=carry_packed.at[plane],
            send_sem=carry_sem.at[plane],
            recv_sem=carry_sem.at[2],
            device_id={"space": place + 1 + plane},
            device_id_type=MESH,
        )

    trade = pltpu.make_async_remote_copy(
        src_ref=carry_packed.at[side],
        dst_ref=carry_packed.at[side],
        send_sem=trade_sem.at[0],
        recv_sem=trade_sem.at[1],
        device_id={"space": partner},
        device_id_type=MESH,
    )

    loads[0].wait()
    loads[1].wait()

    def steps_of(block):
        kept = load(green, block)
        hopping = hop[block]
        ahead = (dot(kept[0], hopping).astype(BF16), dot(kept[1], hopping).astype(BF16))
        behind = (dot_tn(hopping, kept[0]).astype(BF16), dot_tn(hopping, kept[1]).astype(BF16))
        return ahead, behind

    store(conn, load(green, 0), 0)
    for block in range(1, blocks):
        ahead, behind = steps_of(block)
        store(maps, ahead, block)
        store(maps_t, behind, block)
        store(
            conn, sandwich(load(green, block), ahead, load(conn, block - 1), behind), block
        )

    pl.semaphore_wait(
        barrier,
        groups
        + 2 * jnp.where(sends_on, 1, 0).astype(jnp.int32)
        + jnp.where(pair > 0, 1, 0).astype(jnp.int32),
    )

    @pl.when(side == 0)
    def _():
        pair_copies[0].start()

    @pl.when(jnp.logical_or(odd, pair > 0))
    def _():
        ahead, behind = steps_of(0)
        store(maps, ahead, 0)
        store(maps_t, behind, 0)
        for block in range(1, blocks):
            before, before_t = load(maps, block - 1), load(maps_t, block - 1)
            ahead, behind = load(maps, block), load(maps_t, block)
            store(maps, product(ahead, before), block)
            store(maps_t, product(before_t, behind), block)

    @pl.when(jnp.logical_and(side == 0, pair > 0))
    def _():
        pair_copies[1].start()

    loads[2].wait()
    for block in range(blocks):
        for plane in range(2):
            pack(screen_send, plane, block * order, screen[block, plane])
    used = blocks * order
    if groups * chunk > used:
        for ref in (screen_send, green_send):
            ref[:, used:] = jnp.zeros((2, groups * chunk - used, ref.shape[2]), BF16)
    loop(
        1, groups, lambda step: exchange(0, spread(screen_send), screen_recv.at[me], step).start()
    )

    @pl.when(odd)
    def _():
        pair_copies[0].wait_recv()
        below = load(pair_conn)
        for block in reversed(range(blocks)):
            ahead, behind = load(maps, block), load(maps_t, block)
            store(conn, sandwich(load(conn, block), ahead, below, behind), block)

        @pl.when(pair > 0)
        def _():
            pair_copies[1].wait_recv()
            before = load(pair_map)
            for block in range(blocks):
                ahead, behind = load(maps, block), load(maps_t, block)
                store(maps, product(ahead, before), block)
                store(maps_t, product(before, behind, dot_tn), block)

    @pl.when(pair > 0)
    def _():
        @pl.when(side == 0)
        def _():
            pair_copies[0].wait_send()
            pair_copies[1].wait_send()

        pltpu.make_async_remote_copy(
            src_ref=carry_packed.at[side],
            dst_ref=carry_packed.at[side],
            send_sem=carry_sem.at[0],
            recv_sem=carry_sem.at[2],
            device_id={"space": partner},
            device_id_type=MESH,
        ).wait_recv()
        trade.start()
        trade.wait()
        for plane in range(2):
            unpack(carry, (plane,), carry_packed[plane])

    for block in reversed(range(blocks)):

        @pl.when(pair > 0)
        def _():
            ahead, behind = load(maps, block), load(maps_t, block)
            store(conn, sandwich(load(conn, block), ahead, load(carry), behind), block)

        for plane in range(2):
            pack(green_send, plane, block * order, conn[block, plane])
        if block == last:

            @pl.when(sends_on)
            def _():
                for plane in range(2):
                    onward(plane).start()

    loop(1, groups, lambda step: exchange(1, spread(green_send), green_recv.at[me], step).start())
    mine = pl.ds(pl.multiple_of(me * chunk, 16), chunk)
    green_recv[me] = green_send[:, mine]
    screen_recv[me] = screen_send[:, mine]

    whole(0).wait_recv()

    def widen_screen(energy):
        screen_wide[energy] = screen_recv[energy].astype(F32)

    def widen_green(energy):
        green_wide[energy] = green_recv[energy].astype(F32)

    loop(0, groups, widen_screen)
    whole(1).wait_recv()
    loop(0, groups, widen_green)
    scale = 1.0 / math.sqrt(groups)

    def convolved(energy):
        def term(other, total):
            shift = (energy - other + groups) % groups
            g_re, g_im = green_wide[other, 0], green_wide[other, 1]
            s_re, s_im = screen_wide[shift, 0], screen_wide[shift, 1]
            return (
                total[0] + g_re * s_re - g_im * s_im,
                total[1] + g_re * s_im + g_im * s_re,
            )

        zero = jnp.zeros(green_wide.shape[2:], F32)
        total = (zero, zero)
        if groups <= UNROLL:
            for other in range(groups):
                total = term(other, total)
        else:
            total = lax.fori_loop(0, groups, term, total)
        return (total[1] * -scale).astype(BF16), (total[0] * scale).astype(BF16)

    def back(step):
        energy = (me + step) % groups
        real, imag = convolved(energy)
        sigma_send[step, 0] = real
        sigma_send[step, 1] = imag
        exchange(2, lambda to: sigma_send.at[step], spread(sigma_recv)(me), step).start()

    loop(1, groups, back)
    real, imag = convolved(me)
    sigma_recv[0, mine] = real
    sigma_recv[1, mine] = imag
    whole(2).wait_recv()
    for block in range(blocks):
        for plane in range(2):
            unpack(
                out_ref, (0, block, plane), sigma_recv[plane, block * order : (block + 1) * order]
            )

    for index in range(3):
        whole(index).wait_send()

    @pl.when(jnp.logical_and(side == 0, pair == 0))
    def _():
        pair_copies[0].wait_send()

    @pl.when(sends_on)
    def _():
        for plane in range(2):
            onward(plane).wait_send()


def shards(groups, places, iso_green, coupling, screened):
    blocks, order = iso_green.shape[1], iso_green.shape[3]
    tile = order // 3
    width = 2 * tile
    used = blocks * order
    chunk = 16 * -(-used // (16 * groups))
    full = (2, order, order)
    any_spec = pl.BlockSpec(memory_space=pltpu.HBM)
    return pl.pallas_call(
        functools.partial(kernel, groups, places),
        out_shape=jax.ShapeDtypeStruct(iso_green.shape, BF16),
        in_specs=[any_spec] * 3,
        out_specs=pl.BlockSpec(memory_space=pltpu.VMEM),
        scratch_shapes=[
            pltpu.VMEM((blocks, *full), BF16),
            pltpu.VMEM((blocks, order, order), BF16),
            pltpu.VMEM((blocks, *full), BF16),
            pltpu.VMEM((blocks, *full), BF16),
            pltpu.VMEM((blocks, *full), BF16),
            pltpu.VMEM((blocks, *full), BF16),
            pltpu.VMEM(full, BF16),
            pltpu.VMEM(full, BF16),
            pltpu.VMEM((2, order, width), BF16),
            pltpu.VMEM(full, BF16),
            pltpu.VMEM((2, groups * chunk, width), BF16),
            pltpu.VMEM((2, groups * chunk, width), BF16),
            pltpu.VMEM((groups, 2, chunk, width), BF16),
            pltpu.VMEM((groups, 2, chunk, width), BF16),
            pltpu.VMEM((groups, 2, chunk, width), F32),
            pltpu.VMEM((groups, 2, chunk, width), F32),
            pltpu.VMEM((groups, 2, chunk, width), BF16),
            pltpu.VMEM((2, groups * chunk, width), BF16),
            pltpu.SemaphoreType.DMA((3,)),
            pltpu.SemaphoreType.DMA((4,)),
            pltpu.SemaphoreType.DMA((3,)),
            pltpu.SemaphoreType.DMA((2,)),
            pltpu.SemaphoreType.DMA((6,)),
        ],
        compiler_params=pltpu.CompilerParams(
            collective_id=0, has_side_effects=True
        ),
    )(iso_green, coupling, screened)


def solution(mesh):
    groups, places = mesh.shape["energy"], mesh.shape["space"]
    spec = P("energy", "space", None, None, None)
    return jax.shard_map(
        functools.partial(shards, groups, places),
        mesh=mesh,
        in_specs=(spec, P("space", None, None), spec),
        out_specs=spec,
        check_vma=False,
    )
```

```python
import functools
import math

import jax
import jax.numpy as jnp
from jax import lax
from jax.experimental import pallas as pl
from jax.experimental.pallas import tpu as pltpu
from jax.sharding import PartitionSpec as P

MESH = pl.DeviceIdType.MESH
BF16 = jnp.bfloat16
F32 = jnp.float32
UNROLL = 8


def loop(low, high, body):
    if high - low <= UNROLL:
        for step in range(low, high):
            body(step)
    else:

        def one(step, carry):
            body(step)
            return carry

        lax.fori_loop(low, high, one, 0)


def dot(a, b):
    return jnp.dot(a, b, preferred_element_type=F32)


def dot_tn(a, b):
    return lax.dot_general(a, b, (((0,), (0,)), ((), ())), preferred_element_type=F32)


def product(a, b, mul=dot):
    real = mul(a[0], b[0]) - mul(a[1], b[1])
    imag = mul(a[0], b[1]) + mul(a[1], b[0])
    return real, imag


def rounded(pair):
    return pair[0].astype(BF16), pair[1].astype(BF16)


def load(ref, *at):
    return ref[(*at, 0)], ref[(*at, 1)]


def store(ref, pair, *at):
    ref[(*at, 0)] = pair[0].astype(BF16)
    ref[(*at, 1)] = pair[1].astype(BF16)


def sandwich(source, left, inner, right):
    outer = product(left, rounded(product(inner, right)))
    return source[0].astype(F32) + outer[0], source[1].astype(F32) + outer[1]


def pack(ref, plane, start, whole):
    t = whole.shape[0] // 3
    ref[plane, start : start + t] = whole[2 * t :, : 2 * t].astype(BF16)
    ref[plane, start + t : start + 2 * t] = whole[:t, : 2 * t].astype(BF16)
    corner = jnp.concatenate([whole[2 * t :, 2 * t :], whole[t : 2 * t, t : 2 * t]], axis=1)
    ref[plane, start + 2 * t : start + 3 * t] = corner.astype(BF16)


def unpack(ref, at, rows):
    t = rows.shape[0] // 3
    low, top, corner = rows[:t], rows[t : 2 * t], rows[2 * t :]
    flipped = top.astype(F32).T[t:].astype(BF16)
    ref[(*at, slice(2 * t, 3 * t), slice(0, 2 * t))] = low
    ref[(*at, slice(2 * t, 3 * t), slice(2 * t, 3 * t))] = corner[:, :t]
    ref[(*at, slice(0, t), slice(0, 2 * t))] = top
    ref[(*at, slice(t, 2 * t), slice(0, 2 * t))] = jnp.concatenate(
        [flipped, corner[:, t:]], axis=1
    )
    ref[(*at, slice(0, 2 * t), slice(2 * t, 3 * t))] = low.astype(F32).T.astype(BF16)


def kernel(
    groups,
    places,
    iso_ref,
    coupling_ref,
    screened_ref,
    out_ref,
    green,
    hop,
    screen,
    maps,
    maps_t,
    conn,
    pair_conn,
    pair_map,
    carry_packed,
    carry,
    green_send,
    screen_send,
    green_recv,
    screen_recv,
    green_wide,
    screen_wide,
    sigma_send,
    sigma_recv,
    load_sem,
    pair_sem,
    carry_sem,
    trade_sem,
    exchange_sem,
):
    blocks = green.shape[0]
    order = green.shape[-1]
    chunk = green_recv.shape[2]
    last = blocks - 1
    me = lax.axis_index("energy")
    place = lax.axis_index("space")
    pair = place // 2
    side = place % 2
    odd = side == 1
    partner = place + 1 - 2 * side
    pairs = places // 2

    loads = [
        pltpu.make_async_copy(iso_ref.at[0], green, load_sem.at[0]),
        pltpu.make_async_copy(coupling_ref, hop, load_sem.at[1]),
        pltpu.make_async_copy(screened_ref.at[0], screen, load_sem.at[2]),
    ]
    for copy in loads:
        copy.start()

    barrier = pltpu.get_barrier_semaphore()

    def greet(step):
        pl.semaphore_signal(
            barrier, inc=1, device_id={"energy": (me + step) % groups}, device_id_type=MESH
        )

    loop(1, groups, greet)
    pl.semaphore_signal(barrier, inc=1, device_id={"space": partner}, device_id_type=MESH)
    sends_on = jnp.logical_and(odd, pair < pairs - 1)

    @pl.when(sends_on)
    def _():
        for plane in range(2):
            pl.semaphore_signal(
                barrier, inc=1, device_id={"space": place + 1 + plane}, device_id_type=MESH
            )

    @pl.when(pair > 0)
    def _():
        pl.semaphore_signal(barrier, inc=1, device_id={"space": 2 * pair - 1}, device_id_type=MESH)

    def exchange(index, source, target, step):
        to = (me + step) % groups
        return pltpu.make_async_remote_copy(
            src_ref=source(to),
            dst_ref=target,
            send_sem=exchange_sem.at[2 * index],
            recv_sem=exchange_sem.at[2 * index + 1],
            device_id={"energy": to},
            device_id_type=MESH,
        )

    def spread(ref):
        return lambda to: ref.at[:, pl.ds(pl.multiple_of(to * chunk, 16), chunk), :]

    def whole(index):
        part = green_recv.at[pl.ds(0, groups - 1)]
        return pltpu.make_async_remote_copy(
            src_ref=part,
            dst_ref=part,
            send_sem=exchange_sem.at[2 * index],
            recv_sem=exchange_sem.at[2 * index + 1],
            device_id={"energy": (me + 1) % groups},
            device_id_type=MESH,
        )

    pair_copies = [
        pltpu.make_async_remote_copy(
            src_ref=source,
            dst_ref=target,
            send_sem=pair_sem.at[2 * index],
            recv_sem=pair_sem.at[2 * index + 1],
            device_id={"space": partner},
            device_id_type=MESH,
        )
        for index, (source, target) in enumerate(
            [(conn.at[last], pair_conn), (maps.at[last], pair_map)]
        )
    ]

    def onward(plane):
        return pltpu.make_async_remote_copy(
            src_ref=green_send.at[plane, last * order : blocks * order],
            dst_ref=carry_packed.at[plane],
            send_sem=carry_sem.at[plane],
            recv_sem=carry_sem.at[2],
            device_id={"space": place + 1 + plane},
            device_id_type=MESH,
        )

    trade = pltpu.make_async_remote_copy(
        src_ref=carry_packed.at[side],
        dst_ref=carry_packed.at[side],
        send_sem=trade_sem.at[0],
        recv_sem=trade_sem.at[1],
        device_id={"space": partner},
        device_id_type=MESH,
    )

    loads[0].wait()
    loads[1].wait()

    def steps_of(block):
        kept = load(green, block)
        hopping = hop[block]
        ahead = (dot(kept[0], hopping).astype(BF16), dot(kept[1], hopping).astype(BF16))
        behind = (dot_tn(hopping, kept[0]).astype(BF16), dot_tn(hopping, kept[1]).astype(BF16))
        return ahead, behind

    store(conn, load(green, 0), 0)
    for block in range(1, blocks):
        ahead, behind = steps_of(block)
        store(maps, ahead, block)
        store(maps_t, behind, block)
        store(
            conn, sandwich(load(green, block), ahead, load(conn, block - 1), behind), block
        )

    pl.semaphore_wait(
        barrier,
        groups
        + 2 * jnp.where(sends_on, 1, 0).astype(jnp.int32)
        + jnp.where(pair > 0, 1, 0).astype(jnp.int32),
    )

    @pl.when(side == 0)
    def _():
        pair_copies[0].start()

    @pl.when(jnp.logical_or(odd, pair > 0))
    def _():
        ahead, behind = steps_of(0)
        store(maps, ahead, 0)
        store(maps_t, behind, 0)
        for block in range(1, blocks):
            before, before_t = load(maps, block - 1), load(maps_t, block - 1)
            ahead, behind = load(maps, block), load(maps_t, block)
            store(maps, product(ahead, before), block)
            store(maps_t, product(before_t, behind), block)

    @pl.when(jnp.logical_and(side == 0, pair > 0))
    def _():
        pair_copies[1].start()

    loads[2].wait()
    for block in range(blocks):
        for plane in range(2):
            pack(screen_send, plane, block * order, screen[block, plane])
    used = blocks * order
    if groups * chunk > used:
        for ref in (screen_send, green_send):
            ref[:, used:] = jnp.zeros((2, groups * chunk - used, ref.shape[2]), BF16)
    loop(
        1, groups, lambda step: exchange(0, spread(screen_send), screen_recv.at[me], step).start()
    )

    @pl.when(odd)
    def _():
        pair_copies[0].wait_recv()
        below = load(pair_conn)
        for block in reversed(range(blocks)):
            ahead, behind = load(maps, block), load(maps_t, block)
            store(conn, sandwich(load(conn, block), ahead, below, behind), block)

        @pl.when(pair > 0)
        def _():
            pair_copies[1].wait_recv()
            before = load(pair_map)
            for block in range(blocks):
                ahead, behind = load(maps, block), load(maps_t, block)
                store(maps, product(ahead, before), block)
                store(maps_t, product(before, behind, dot_tn), block)

    @pl.when(pair > 0)
    def _():
        @pl.when(side == 0)
        def _():
            pair_copies[0].wait_send()
            pair_copies[1].wait_send()

        pltpu.make_async_remote_copy(
            src_ref=carry_packed.at[side],
            dst_ref=carry_packed.at[side],
            send_sem=carry_sem.at[0],
            recv_sem=carry_sem.at[2],
            device_id={"space": partner},
            device_id_type=MESH,
        ).wait_recv()
        trade.start()
        trade.wait()
        for plane in range(2):
            unpack(carry, (plane,), carry_packed[plane])

    for block in reversed(range(blocks)):

        @pl.when(pair > 0)
        def _():
            ahead, behind = load(maps, block), load(maps_t, block)
            store(conn, sandwich(load(conn, block), ahead, load(carry), behind), block)

        for plane in range(2):
            pack(green_send, plane, block * order, conn[block, plane])
        if block == last:

            @pl.when(sends_on)
            def _():
                for plane in range(2):
                    onward(plane).start()

    loop(1, groups, lambda step: exchange(1, spread(green_send), green_recv.at[me], step).start())
    mine = pl.ds(pl.multiple_of(me * chunk, 16), chunk)
    green_recv[me] = green_send[:, mine]
    screen_recv[me] = screen_send[:, mine]

    whole(0).wait_recv()

    def widen_screen(energy):
        screen_wide[energy] = screen_recv[energy].astype(F32)

    def widen_green(energy):
        green_wide[energy] = green_recv[energy].astype(F32)

    loop(0, groups, widen_screen)
    whole(1).wait_recv()
    loop(0, groups, widen_green)
    scale = 1.0 / math.sqrt(groups)

    def convolved(energy):
        def term(other, total):
            shift = (energy - other + groups) % groups
            g_re, g_im = green_wide[other, 0], green_wide[other, 1]
            s_re, s_im = screen_wide[shift, 0], screen_wide[shift, 1]
            return (
                total[0] + g_re * s_re - g_im * s_im,
                total[1] + g_re * s_im + g_im * s_re,
            )

        zero = jnp.zeros(green_wide.shape[2:], F32)
        total = (zero, zero)
        if groups <= UNROLL:
            for other in range(groups):
                total = term(other, total)
        else:
            total = lax.fori_loop(0, groups, term, total)
        return (total[1] * -scale).astype(BF16), (total[0] * scale).astype(BF16)

    def back(step):
        energy = (me + step) % groups
        real, imag = convolved(energy)
        sigma_send[step, 0] = real
        sigma_send[step, 1] = imag
        exchange(2, lambda to: sigma_send.at[step], spread(sigma_recv)(me), step).start()

    loop(1, groups, back)
    real, imag = convolved(me)
    sigma_recv[0, mine] = real
    sigma_recv[1, mine] = imag
    whole(2).wait_recv()
    out_ref[...] = sigma_recv[:, :used]

    for index in range(3):
        whole(index).wait_send()

    @pl.when(jnp.logical_and(side == 0, pair == 0))
    def _():
        pair_copies[0].wait_send()

    @pl.when(sends_on)
    def _():
        for plane in range(2):
            onward(plane).wait_send()


def unfold(packed_ref, out_ref):
    blocks, order = out_ref.shape[1], out_ref.shape[-1]
    for block in range(blocks):
        for plane in range(2):
            unpack(
                out_ref, (0, block, plane), packed_ref[plane, block * order : (block + 1) * order]
            )


def shards(groups, places, iso_green, coupling, screened):
    blocks, order = iso_green.shape[1], iso_green.shape[3]
    tile = order // 3
    width = 2 * tile
    used = blocks * order
    chunk = 16 * -(-used // (16 * groups))
    full = (2, order, order)
    any_spec = pl.BlockSpec(memory_space=pltpu.HBM)
    packed = pl.pallas_call(
        functools.partial(kernel, groups, places),
        out_shape=jax.ShapeDtypeStruct((2, used, width), BF16),
        in_specs=[any_spec] * 3,
        out_specs=pl.BlockSpec(memory_space=pltpu.VMEM),
        scratch_shapes=[
            pltpu.VMEM((blocks, *full), BF16),
            pltpu.VMEM((blocks, order, order), BF16),
            pltpu.VMEM((blocks, *full), BF16),
            pltpu.VMEM((blocks, *full), BF16),
            pltpu.VMEM((blocks, *full), BF16),
            pltpu.VMEM((blocks, *full), BF16),
            pltpu.VMEM(full, BF16),
            pltpu.VMEM(full, BF16),
            pltpu.VMEM((2, order, width), BF16),
            pltpu.VMEM(full, BF16),
            pltpu.VMEM((2, groups * chunk, width), BF16),
            pltpu.VMEM((2, groups * chunk, width), BF16),
            pltpu.VMEM((groups, 2, chunk, width), BF16),
            pltpu.VMEM((groups, 2, chunk, width), BF16),
            pltpu.VMEM((groups, 2, chunk, width), F32),
            pltpu.VMEM((groups, 2, chunk, width), F32),
            pltpu.VMEM((groups, 2, chunk, width), BF16),
            pltpu.VMEM((2, groups * chunk, width), BF16),
            pltpu.SemaphoreType.DMA((3,)),
            pltpu.SemaphoreType.DMA((4,)),
            pltpu.SemaphoreType.DMA((3,)),
            pltpu.SemaphoreType.DMA((2,)),
            pltpu.SemaphoreType.DMA((6,)),
        ],
        compiler_params=pltpu.CompilerParams(
            collective_id=0, has_side_effects=True
        ),
    )(iso_green, coupling, screened)
    return pl.pallas_call(
        unfold,
        out_shape=jax.ShapeDtypeStruct(iso_green.shape, BF16),
        in_specs=[pl.BlockSpec(memory_space=pltpu.VMEM)],
        out_specs=pl.BlockSpec(memory_space=pltpu.VMEM),
    )(packed)


def solution(mesh):
    groups, places = mesh.shape["energy"], mesh.shape["space"]
    spec = P("energy", "space", None, None, None)
    return jax.shard_map(
        functools.partial(shards, groups, places),
        mesh=mesh,
        in_specs=(spec, P("space", None, None), spec),
        out_specs=spec,
        check_vma=False,
    )
```
